128 devices in a mesh: row: 8 (over z_hi, x), col: 8 (over y, z_lo), pair: 2 (over core).
Axes of the slice: x: 4, y: 4, z: 4 (z_hi: 2, z_lo: 2; z = z_hi * 2 + z_lo), core: 2. Of those that a mesh axis runs over, the one named last changes fastest.
Arguments:
- amplitudes: bfloat16 [512, 256], P(('row', 'col'), 'pair'), may hold values from -8 to 8
- integrals: bfloat16 [1400, 1400, 256], P('row', 'col', 'pair'), may hold values from -0.375 to 0.375
- irrep_sizes: int32 [8], replicated, may hold values from 1 to 350, 1400 in all
- pair_irrep: int32 [512], replicated, may hold values from 0 to 7
Outputs:
- residual: bfloat16 [1400, 1400, 512], P('row', 'col', 'pair')
The draws below stay inside these ranges and needn't reach their ends.
Inputs may be any that keep to these rules, and one draw needn't show every extreme that they name: `irrep_sizes`: the sizes of the 8 symmetry blocks of the virtual orbitals, which follow one another in orbital order and sum to 1400.
All inputs are finite; a program needn't handle non-finite values.
Results may differ from the reference program's by a relative error of at most 0.001.
Values may be sent and summed in bfloat16 or wider, within the bound.
A program may use at most 256 MiB of HBM per device.

```python
import math
import jax
import jax.numpy as jnp
import numpy as np
from jax import lax

NV = 1400
NIRREP = 8
P_SIZE = 512
K = 256


def touch_ends(array, stream_key, low, top_value):
    spot = [jax.random.randint(jax.random.fold_in(stream_key, axis), (), 0, length) for axis, length in enumerate(array.shape)]
    main_axis = array.shape.index(max(array.shape))
    neighbour = spot[:main_axis] + [(spot[main_axis] + 1) % array.shape[main_axis]] + spot[main_axis + 1:]
    return array.at[tuple(spot)].set(low).at[tuple(neighbour)].set(top_value)


def block_scale(stream_key, extent, split, low, largest):
    gain, own = 1.0, jax.random.fold_in(stream_key, 6)
    for position, shards_of in split:
        heights = jnp.exp(jax.random.uniform(jax.random.fold_in(own, position), (shards_of,), jnp.float32, low / len(split), largest / len(split)))
        gain = gain * jnp.repeat(heights, extent[position] // shards_of).reshape([-1 if axis == position else 1 for axis in range(len(extent))])
    return gain


def profile(amount, total, limit, skew):
    portions = [(1 << 20) // math.isqrt(rank ** skew) + 1 for rank in range(2, amount + 1)]
    rest, holding = total - limit - (amount - 1), [1] * (amount - 1)
    while rest > 0:
        candidates = [i for i in range(amount - 1) if holding[i] < limit]
        mass, remaining = sum([portions[i] for i in candidates]), rest
        for i in candidates:
            extra = min(limit - holding[i], max(1, remaining * portions[i] // mass), rest)
            holding[i] = holding[i] + extra
            rest = rest - extra
    return np.array([limit] + holding)


def ragged(rng, number_of, total, reach, lean):
    if number_of == 2:
        one = jax.random.randint(rng, (), max(1, total - reach), min(reach, total - 1) + 1)
        return jnp.stack([one, total - one])
    sizes = jnp.asarray(profile(number_of, total, reach, lean), jnp.int32)
    twos = (number_of - 1) // 2
    giver, taker = sizes[1:1 + 2 * twos:2], sizes[2:2 + 2 * twos:2]
    margin = jnp.minimum(giver - 1, reach - taker)
    shifted = jax.random.randint(jax.random.fold_in(rng, 1), (twos,), 0, 1 << 20) % (margin + 1)
    sizes = sizes.at[1:1 + 2 * twos:2].set(giver - shifted).at[2:2 + 2 * twos:2].set(taker + shifted)
    return sizes[jax.random.permutation(jax.random.fold_in(rng, 2), number_of)]


def scatter_about(own_key, extent, scale, limit, split=(), held_as=jnp.bfloat16):
    array = scale * jax.random.normal(own_key, extent, jnp.float32)
    if split:
        array = array * block_scale(own_key, extent, split, -0.22, 0.18)
    return jnp.clip(array, -limit, limit).astype(held_as)


def setup_inputs(seed: int = 0) -> dict:
    splits = jax.random.split(jax.random.key(seed), 5)
    return {
        "amplitudes": scatter_about(splits[0], (P_SIZE, K), 2.0, 8.0, ((0, 64), (1, 2))),
        "integrals": scatter_about(splits[1], (NV, NV, K), K ** -0.5, 0.375, ((0, 8), (1, 8), (2, 2))),
        "irrep_sizes": ragged(splits[2], NIRREP, NV, NV // 4, 1).astype(jnp.int32),
        "pair_irrep": touch_ends(jax.random.randint(splits[3], (P_SIZE,), 0, NIRREP), jax.random.fold_in(splits[3], 1), 0, NIRREP - 1).astype(jnp.int32),
    }


def irrep_table(irrep_sizes):
    block_ends = jnp.cumsum(irrep_sizes)
    virtual = jnp.arange(NV, dtype=jnp.int32)
    return jnp.sum((virtual[:, None] >= block_ends[None, :]).astype(jnp.int32), axis=1)


def reference(amplitudes, integrals, irrep_sizes, pair_irrep):
    irrep = irrep_table(irrep_sizes)

    def one_orbital(orbital):
        slab_rows = lax.dynamic_index_in_dim(integrals, orbital, axis=0, keepdims=False)
        ladder = 0.5 * lax.dot_general(slab_rows, amplitudes, (((1,), (1,)), ((), ())), preferred_element_type=jnp.float32)
        product_irrep = jnp.bitwise_xor(irrep[orbital], irrep)
        allowed = product_irrep[:, None] == pair_irrep[None, :]
        return jnp.where(allowed, ladder, jnp.zeros_like(ladder)).astype(jnp.bfloat16)

    return lax.map(one_orbital, jnp.arange(NV, dtype=jnp.int32))
```

```python
import functools

import jax
import jax.numpy as jnp
from jax import lax
from jax.experimental import pallas as pl
from jax.experimental.pallas import tpu as pltpu
from jax.sharding import PartitionSpec as P

MESH = pl.DeviceIdType.MESH


def exchange_kernel(
    n_row, n_col, amp_ref, integ_ref, sizes_ref, pairs_ref,
    other_ref, own_ref, weights_ref, masks_ref,
    part, gathered, crossed,
    slab_send, slab_recv, own_sem, col_send, col_recv, row_send, row_recv, pair_send, pair_recv,
):
    row, col, pair = lax.axis_index("row"), lax.axis_index("col"), lax.axis_index("pair")
    partner = (row, col, 1 - pair)
    col_peers = [(row, lax.rem(col + d, n_col), pair) for d in range(1, n_col)]
    row_peers = [(lax.rem(row + d, n_row), col, pair) for d in range(1, n_row)]
    block = amp_ref.shape[0]
    strip = n_col * block
    half = n_row * strip // 2

    barrier = pltpu.get_barrier_semaphore()
    peers = [partner] + col_peers + row_peers
    for peer in peers:
        pl.semaphore_signal(barrier, inc=1, device_id=peer, device_id_type=MESH)
    own_copy = pltpu.make_async_copy(integ_ref, own_ref, own_sem)
    own_copy.start()
    part[...] = amp_ref[...].astype(jnp.float32)
    pl.semaphore_wait(barrier, len(peers))

    slab = pltpu.make_async_remote_copy(
        integ_ref, other_ref, slab_send, slab_recv, device_id=partner, device_id_type=MESH
    )
    slab.start()

    mine = pl.ds(pl.multiple_of((row * n_col + col) * block, block), block)
    col_copies = [
        pltpu.make_async_remote_copy(
            part, gathered.at[mine], col_send.at[d], col_recv.at[d], device_id=peer, device_id_type=MESH
        )
        for d, peer in enumerate(col_peers)
    ]
    for copy in col_copies:
        copy.start()
    gathered[mine] = part[...]
    for copy in col_copies:
        copy.wait()

    line = pl.ds(pl.multiple_of(row * strip, strip), strip)
    row_copies = [
        pltpu.make_async_remote_copy(
            gathered.at[line], gathered.at[line], row_send.at[d], row_recv.at[d], device_id=peer, device_id_type=MESH
        )
        for d, peer in enumerate(row_peers)
    ]
    for copy in row_copies:
        copy.start()
    for copy in row_copies:
        copy.wait()

    theirs = pl.ds(pl.multiple_of((1 - pair) * half, half), half)
    ours = pl.ds(pl.multiple_of(pair * half, half), half)
    cross = pltpu.make_async_remote_copy(
        gathered.at[theirs], crossed, pair_send, pair_recv, device_id=partner, device_id_type=MESH
    )
    cross.start()

    rows, cols = masks_ref.shape[1], masks_ref.shape[2]
    orbital = col * integ_ref.shape[1] + lax.broadcasted_iota(jnp.int32, (rows, cols), 0)
    irrep = jnp.zeros((rows, cols), jnp.int32)
    end = jnp.int32(0)
    for j in range(masks_ref.shape[0]):
        end = end + sizes_ref[j]
        irrep = irrep + (orbital >= end).astype(jnp.int32)
    wanted = irrep ^ pairs_ref[pl.ds(pair, 1), :]
    for i in range(masks_ref.shape[0]):
        masks_ref[i] = jnp.where(wanted == i, 0.5, 0.0).astype(jnp.bfloat16)

    depth = crossed.shape[1]
    weights_ref[:depth] = gathered[ours].T.astype(jnp.bfloat16)
    cross.wait()
    weights_ref[depth:] = crossed[...].T.astype(jnp.bfloat16)
    own_copy.wait()
    slab.wait()


def ladder_kernel(chunk, own_ref, other_ref, weights_ref, masks_ref, sizes_ref, out_ref, staged, sems):
    rows, cols = own_ref.shape[0], own_ref.shape[1]
    first = lax.axis_index("row") * rows
    ends, end = [], jnp.int32(0)
    for j in range(masks_ref.shape[0]):
        end = end + sizes_ref[j]
        ends.append(end)

    def copy(c):
        span = pl.ds(c * chunk, chunk)
        return pltpu.make_async_copy(staged.at[span], out_ref.at[span], sems.at[c])

    @pl.loop(0, rows // chunk)
    def _(c):
        for i in range(chunk):
            a = c * chunk + i
            irrep = jnp.int32(0)
            for e in ends:
                irrep = irrep + (first + a >= e).astype(jnp.int32)
            slab = jnp.concatenate([own_ref[a], other_ref[a]], axis=1)
            ladder = jnp.dot(slab, weights_ref[...], preferred_element_type=jnp.float32)
            staged[a] = ladder.astype(jnp.bfloat16) * masks_ref[irrep][:cols]
        copy(c).start()

    @pl.loop(0, rows // chunk)
    def _(c):
        copy(c).wait()


def solution(mesh):
    n_row, n_col = mesh.shape["row"], mesh.shape["col"]

    def body(amplitudes, integrals, irrep_sizes, pair_irrep):
        rows, cols, depth = integrals.shape
        n_irrep = irrep_sizes.shape[0]
        n_pairs = pair_irrep.shape[0]
        half = n_pairs // 2
        block = amplitudes.shape[0]
        padded = (cols + 15) // 16 * 16
        vmem, smem = pl.BlockSpec(memory_space=pltpu.VMEM), pl.BlockSpec(memory_space=pltpu.SMEM)
        hbm = pl.BlockSpec(memory_space=pltpu.HBM)
        dma = pltpu.SemaphoreType.DMA
        other, own, weights, masks = pl.pallas_call(
            functools.partial(exchange_kernel, n_row, n_col),
            out_shape=(
                pltpu.VMEM(integrals.shape, jnp.bfloat16),
                pltpu.VMEM(integrals.shape, jnp.bfloat16),
                pltpu.VMEM((2 * depth, half), jnp.bfloat16),
                pltpu.VMEM((n_irrep, padded, half), jnp.bfloat16),
            ),
            in_specs=[vmem, hbm, smem, vmem],
            out_specs=(vmem,) * 4,
            scratch_shapes=[
                pltpu.VMEM((block, depth), jnp.float32),
                pltpu.VMEM((n_pairs, depth), jnp.float32),
                pltpu.VMEM((half, depth), jnp.float32),
                dma, dma, dma,
                dma((n_col - 1,)), dma((n_col - 1,)), dma((n_row - 1,)), dma((n_row - 1,)), dma, dma,
            ],
            compiler_params=pltpu.CompilerParams(
                collective_id=0, has_side_effects=True, vmem_limit_bytes=24 << 20
            ),
            name="exchange",
        )(amplitudes, pltpu.with_memory_space_constraint(integrals, pltpu.HBM), irrep_sizes, pair_irrep.reshape(2, half))
        chunk = 7
        return pl.pallas_call(
            functools.partial(ladder_kernel, chunk),
            out_shape=jax.ShapeDtypeStruct((rows, cols, half), jnp.bfloat16),
            in_specs=[vmem, vmem, vmem, vmem, smem],
            out_specs=hbm,
            scratch_shapes=[pltpu.VMEM((rows, cols, half), jnp.bfloat16), dma((rows // chunk,))],
            compiler_params=pltpu.CompilerParams(vmem_limit_bytes=24 << 20),
            name="ladder",
        )(own, other, weights, masks, irrep_sizes)

    return jax.shard_map(
        body,
        mesh=mesh,
        in_specs=(P(("row", "col"), "pair"), P("row", "col", "pair"), P(), P()),
        out_specs=P("row", "col", "pair"),
        check_vma=False,
    )
```

```python
import functools

import jax
import jax.numpy as jnp
from jax import lax
from jax.experimental import pallas as pl
from jax.experimental.pallas import tpu as pltpu
from jax.sharding import PartitionSpec as P

MESH = pl.DeviceIdType.MESH


def exchange_kernel(
    n_row, n_col, amp_hbm, integ_ref, sizes_hbm, pairs_hbm,
    other_ref, own_ref, weights_ref, masks_ref, ends_ref,
    amp_ref, sizes_ref, pairs_ref, part, strip, factors,
    ready, go, slab_send, slab_recv, own_sem, in_sems, col_send, col_recv, row_send, row_recv,
):
    row, col, pair = lax.axis_index("row"), lax.axis_index("col"), lax.axis_index("pair")
    partner = (row, col, 1 - pair)
    block = amp_ref.shape[0]
    rows_of_strip = n_col * block
    half_rows = n_row // 2
    half = half_rows * rows_of_strip
    target_pair = row // half_rows
    slot = pair * half_rows + lax.rem(row, half_rows)
    n_slots = 2 * half_rows

    barrier = pltpu.get_barrier_semaphore()

    @pl.when(pair == 0)
    def _():
        pl.semaphore_signal(barrier, inc=1, device_id=partner, device_id_type=MESH)

    fetches = [
        pltpu.make_async_copy(amp_hbm, amp_ref, in_sems.at[0]),
        pltpu.make_async_copy(sizes_hbm, sizes_ref, in_sems.at[1]),
        pltpu.make_async_copy(pairs_hbm, pairs_ref, in_sems.at[2]),
    ]
    for fetch in fetches:
        fetch.start()

    @pl.when(pair == 1)
    def _():
        pl.semaphore_wait(barrier, 1)
        pl.semaphore_signal(ready, inc=1, device_id=partner, device_id_type=MESH)

    @pl.when(pair == 0)
    def _():
        pl.semaphore_wait(ready, 1)

    slab = pltpu.make_async_remote_copy(
        integ_ref, other_ref, slab_send, slab_recv, device_id=partner, device_id_type=MESH
    )
    slab.start()
    own_copy = pltpu.make_async_copy(integ_ref, own_ref, own_sem)
    own_copy.start()

    @pl.when(pair == 0)
    def _():
        peers = [(row, lax.rem(col + d, n_col), 0) for d in range(1, n_col)]
        peers += [(lax.rem(row + d, n_row), col, 0) for d in range(1, n_row)]
        for peer in peers:
            pl.semaphore_signal(barrier, inc=1, device_id=peer, device_id_type=MESH)
        pl.semaphore_wait(barrier, len(peers))
        pl.semaphore_signal(go, inc=1, device_id=partner, device_id_type=MESH)

    fetches[0].wait()
    part[...] = amp_ref[...].astype(jnp.float32)

    @pl.when(pair == 1)
    def _():
        pl.semaphore_wait(go, 1)

    mine = pl.ds(pl.multiple_of(col * block, block), block)
    col_copies = [
        pltpu.make_async_remote_copy(
            part, strip.at[mine], col_send.at[d - 1], col_recv.at[d - 1],
            device_id=(row, lax.rem(col + d, n_col), pair), device_id_type=MESH,
        )
        for d in range(1, n_col)
    ]
    for copy in col_copies:
        copy.start()
    strip[mine] = part[...]
    for copy in col_copies:
        copy.wait_recv()

    def place(s):
        return factors.at[pl.ds(pl.multiple_of(s * rows_of_strip, rows_of_strip), rows_of_strip)]

    def row_copy(d):
        return pltpu.make_async_remote_copy(
            strip, place(slot), row_send.at[d], row_recv.at[slot],
            device_id=(lax.rem(row + d, n_row), col, target_pair), device_id_type=MESH,
        )

    for d in range(1, n_row):
        row_copy(d).start()

    @pl.when(target_pair != pair)
    def _():
        row_copy(0).start()

    @pl.when(target_pair == pair)
    def _():
        place(slot)[...] = strip[...]

    for fetch in fetches[1:]:
        fetch.wait()
    rows, cols = masks_ref.shape[1], masks_ref.shape[2]
    orbital = col * integ_ref.shape[1] + lax.broadcasted_iota(jnp.int32, (rows, cols), 0)
    irrep = jnp.zeros((rows, cols), jnp.int32)
    end = jnp.int32(0)
    for j in range(masks_ref.shape[0]):
        end = end + sizes_ref[j]
        ends_ref[j] = end
        irrep = irrep + (orbital >= end).astype(jnp.int32)
    wanted = irrep ^ pairs_ref[pl.ds(pl.multiple_of(pair * half, half), half)][None, :]
    for i in range(masks_ref.shape[0]):
        masks_ref[i] = jnp.where(wanted == i, 0.5, 0.0).astype(jnp.bfloat16)

    for s in range(n_slots):
        sender_pair, sender_row = s // half_rows, pair * half_rows + s % half_rows

        @pl.when(jnp.logical_or(sender_pair != pair, sender_row != row))
        def _():
            pltpu.make_async_remote_copy(
                strip, place(s), row_send.at[0], row_recv.at[s], device_id=partner, device_id_type=MESH
            ).wait_recv()

    depth = strip.shape[1]
    weights_ref[pl.ds(pl.multiple_of(0, depth), depth)] = (
        factors[pl.ds(pl.multiple_of(pair * half, half), half)].T.astype(jnp.bfloat16)
    )
    weights_ref[pl.ds(depth, depth)] = (
        factors[pl.ds(pl.multiple_of((1 - pair) * half, half), half)].T.astype(jnp.bfloat16)
    )

    for copy in col_copies:
        copy.wait_send()
    for d in range(1, n_row):
        row_copy(d).wait_send()

    @pl.when(target_pair != pair)
    def _():
        row_copy(0).wait_send()

    own_copy.wait()
    slab.wait()


def ladder_kernel(unroll, group, own_ref, other_ref, weights_ref, masks_ref, ends_ref, out_ref, staged, sems):
    rows, cols = own_ref.shape[0], own_ref.shape[1]
    first = lax.axis_index("row") * rows
    padded = masks_ref.shape[1]
    ends = [ends_ref[j] for j in range(masks_ref.shape[0])]

    def copy(c):
        span = pl.ds(c * group, group)
        return pltpu.make_async_copy(staged.at[span], out_ref.at[span], sems.at[c])

    def tall(slab):
        return jnp.concatenate([slab, jnp.zeros((padded - cols, slab.shape[1]), slab.dtype)], axis=0)

    @pl.loop(0, rows // unroll)
    def _(step):
        for g in range(unroll // group):
            c = step * (unroll // group) + g
            slabs = [
                jnp.concatenate([tall(own_ref[c * group + i]), tall(other_ref[c * group + i])], axis=1)
                for i in range(group)
            ]
            ladder = jnp.dot(
                jnp.concatenate(slabs, axis=0), weights_ref[...], preferred_element_type=jnp.float32
            )
            for i in range(group):
                a = c * group + i
                irrep = jnp.int32(0)
                for e in ends:
                    irrep = irrep + (first + a >= e).astype(jnp.int32)
                kept = ladder[i * padded : (i + 1) * padded].astype(jnp.bfloat16) * masks_ref[irrep]
                staged[a] = kept[:cols]
            copy(c).start()

    @pl.loop(0, rows // group)
    def _(c):
        copy(c).wait()


def solution(mesh):
    n_row, n_col = mesh.shape["row"], mesh.shape["col"]

    def body(amplitudes, integrals, irrep_sizes, pair_irrep):
        rows, cols, depth = integrals.shape
        n_irrep = irrep_sizes.shape[0]
        n_pairs = pair_irrep.shape[0]
        half = n_pairs // 2
        block = amplitudes.shape[0]
        padded = (cols + 15) // 16 * 16
        vmem, smem = pl.BlockSpec(memory_space=pltpu.VMEM), pl.BlockSpec(memory_space=pltpu.SMEM)
        hbm = pl.BlockSpec(memory_space=pltpu.HBM)
        dma, regular = pltpu.SemaphoreType.DMA, pltpu.SemaphoreType.REGULAR
        inputs = [
            pltpu.with_memory_space_constraint(x, pltpu.HBM)
            for x in (amplitudes, integrals, irrep_sizes, pair_irrep)
        ]
        other, own, weights, masks, ends = pl.pallas_call(
            functools.partial(exchange_kernel, n_row, n_col),
            out_shape=(
                pltpu.VMEM(integrals.shape, jnp.bfloat16),
                pltpu.VMEM(integrals.shape, jnp.bfloat16),
                pltpu.VMEM((2 * depth, half), jnp.bfloat16),
                pltpu.VMEM((n_irrep, padded, half), jnp.bfloat16),
                pltpu.SMEM((n_irrep,), jnp.int32),
            ),
            in_specs=[hbm] * 4,
            out_specs=(vmem,) * 4 + (smem,),
            scratch_shapes=[
                pltpu.VMEM((block, depth), jnp.bfloat16),
                pltpu.SMEM((n_irrep,), jnp.int32),
                pltpu.VMEM((n_pairs,), jnp.int32),
                pltpu.VMEM((block, depth), jnp.float32),
                pltpu.VMEM((n_col * block, depth), jnp.float32),
                pltpu.VMEM((n_pairs, depth), jnp.float32),
                regular, regular, dma, dma, dma, dma((3,)),
                dma((n_col - 1,)), dma((n_col - 1,)), dma((n_row,)), dma((n_row,)),
            ],
            compiler_params=pltpu.CompilerParams(
                collective_id=0, has_side_effects=True, vmem_limit_bytes=24 << 20
            ),
            name="exchange",
        )(*inputs)
        unroll, group = 35, 7
        return pl.pallas_call(
            functools.partial(ladder_kernel, unroll, group),
            out_shape=jax.ShapeDtypeStruct((rows, cols, half), jnp.bfloat16),
            in_specs=[vmem, vmem, vmem, vmem, smem],
            out_specs=hbm,
            scratch_shapes=[pltpu.VMEM((rows, cols, half), jnp.bfloat16), dma((rows // group,))],
            compiler_params=pltpu.CompilerParams(vmem_limit_bytes=24 << 20),
            name="ladder",
        )(own, other, weights, masks, ends)

    return jax.shard_map(
        body,
        mesh=mesh,
        in_specs=(P(("row", "col"), "pair"), P("row", "col", "pair"), P(), P()),
        out_specs=P("row", "col", "pair"),
        check_vma=False,
    )
```

```python
import functools

import jax
import jax.numpy as jnp
from jax import lax
from jax.experimental import pallas as pl
from jax.experimental.pallas import tpu as pltpu
from jax.sharding import PartitionSpec as P

MESH = pl.DeviceIdType.MESH


def exchange_kernel(
    n_row, n_col, amp_hbm, integ_ref, sizes_hbm, pairs_hbm,
    other_ref, own_ref, weights_ref, masks_ref, ends_ref,
    amp_ref, sizes_ref, pairs_ref, chip_block, packed, factors,
    ready, go, slab_send, slab_recv, own_sem, in_sems, swap_send, swap_recv, wide_send, wide_recv,
):
    row, col, pair = lax.axis_index("row"), lax.axis_index("col"), lax.axis_index("pair")
    partner = (row, col, 1 - pair)
    block, depth = amp_ref.shape
    half_rows = n_row // 2
    n_slots = half_rows * n_col
    tall = 2 * block
    target_pair = row // half_rows
    slot = lax.rem(row, half_rows) * n_col + col

    barrier = pltpu.get_barrier_semaphore()

    @pl.when(pair == 0)
    def _():
        pl.semaphore_signal(barrier, inc=1, device_id=partner, device_id_type=MESH)

    fetches = [
        pltpu.make_async_copy(amp_hbm, amp_ref, in_sems.at[0]),
        pltpu.make_async_copy(sizes_hbm, sizes_ref, in_sems.at[1]),
        pltpu.make_async_copy(pairs_hbm, pairs_ref, in_sems.at[2]),
    ]
    for fetch in fetches:
        fetch.start()

    @pl.when(pair == 1)
    def _():
        pl.semaphore_wait(barrier, 1)
        pl.semaphore_signal(ready, inc=1, device_id=partner, device_id_type=MESH)

    @pl.when(pair == 0)
    def _():
        pl.semaphore_wait(ready, 1)

    slab = pltpu.make_async_remote_copy(
        integ_ref, other_ref, slab_send, slab_recv, device_id=partner, device_id_type=MESH
    )
    slab.start()

    fetches[0].wait()
    mine = pl.ds(pl.multiple_of(pair * block, block), block)
    chip_block[mine] = amp_ref[...].astype(jnp.float32)
    swap = pltpu.make_async_remote_copy(
        chip_block.at[mine], chip_block.at[mine], swap_send, swap_recv, device_id=partner, device_id_type=MESH
    )
    swap.start()

    for m in range(half_rows):
        for o in range(n_col):
            source_row = pair * half_rows + lax.rem(row + m, half_rows)
            source = (source_row, lax.rem(col + o, n_col), 0)

            def tell():
                pl.semaphore_signal(barrier, inc=1, device_id=source, device_id_type=MESH)

            if m == 0 and o == 0:
                pl.when(target_pair != pair)(tell)
            else:
                tell()

    own_copy = pltpu.make_async_copy(integ_ref, own_ref, own_sem)
    own_copy.start()

    swap.wait_recv()
    packed[...] = chip_block[...].astype(jnp.bfloat16)

    @pl.when(pair == 0)
    def _():
        pl.semaphore_wait(barrier, n_row * n_col - 1)
        pl.semaphore_signal(go, inc=1, device_id=partner, device_id_type=MESH)

    @pl.when(pair == 1)
    def _():
        pl.semaphore_wait(go, 1)

    def place(s):
        return factors.at[pl.ds(pl.multiple_of(s * tall, tall), tall)]

    def wide(i):
        d_row, d_col = i // (n_col // 2), 2 * (i % (n_col // 2))
        target = (lax.rem(row + d_row, n_row), lax.rem(col + pair + d_col, n_col), target_pair)
        return pltpu.make_async_remote_copy(
            packed, place(slot), wide_send.at[i], wide_recv.at[slot], device_id=target, device_id_type=MESH
        )

    n_targets = n_row * n_col // 2
    for i in range(1, n_targets):
        wide(i).start()

    @pl.when(jnp.logical_or(pair == 1, target_pair == 1))
    def _():
        wide(0).start()

    @pl.when(jnp.logical_and(pair == 0, target_pair == 0))
    def _():
        place(slot)[...] = packed[...]

    for fetch in fetches[1:]:
        fetch.wait()
    half = weights_ref.shape[1]
    rows, cols = masks_ref.shape[1], masks_ref.shape[2]
    orbital = col * integ_ref.shape[1] + lax.broadcasted_iota(jnp.int32, (rows, cols), 0)
    irrep = jnp.zeros((rows, cols), jnp.int32)
    end = jnp.int32(0)
    for j in range(masks_ref.shape[0]):
        end = end + sizes_ref[j]
        ends_ref[j] = end
        irrep = irrep + (orbital >= end).astype(jnp.int32)
    wanted = irrep ^ pairs_ref[pl.ds(pl.multiple_of(pair * half, half), half)][None, :]
    for i in range(masks_ref.shape[0]):
        masks_ref[i] = jnp.where(wanted == i, 0.5, 0.0).astype(jnp.bfloat16)

    for s in range(n_slots):

        def arrive():
            pltpu.make_async_remote_copy(
                packed, place(s), wide_send.at[0], wide_recv.at[s], device_id=partner, device_id_type=MESH
            ).wait_recv()

        here = jnp.logical_and(jnp.logical_and(pair == 0, target_pair == 0), slot == s)
        pl.when(jnp.logical_not(here))(arrive)

    both = factors[...].astype(jnp.float32).reshape(n_slots, 2, block, depth)
    for k in range(2):
        part = both[:, k].reshape(half, depth).T.astype(jnp.bfloat16)
        weights_ref[pl.ds(pl.multiple_of(lax.rem(pair + k, 2) * depth, depth), depth)] = part

    swap.wait_send()
    for i in range(1, n_targets):
        wide(i).wait_send()

    @pl.when(jnp.logical_or(pair == 1, target_pair == 1))
    def _():
        wide(0).wait_send()

    own_copy.wait()
    slab.wait()


def ladder_kernel(chunk, own_ref, other_ref, weights_ref, masks_ref, ends_ref, out_ref, staged, sems):
    rows, cols = own_ref.shape[0], own_ref.shape[1]
    first = lax.axis_index("row") * rows
    ends = [ends_ref[j] for j in range(masks_ref.shape[0])]

    def copy(c):
        span = pl.ds(c * chunk, chunk)
        return pltpu.make_async_copy(staged.at[span], out_ref.at[span], sems.at[c])

    for a in range(rows):
        irrep = jnp.int32(0)
        for e in ends:
            irrep = irrep + (first + a >= e).astype(jnp.int32)
        slab = jnp.concatenate([own_ref[a], other_ref[a]], axis=1)
        ladder = jnp.dot(slab, weights_ref[...], preferred_element_type=jnp.float32)
        staged[a] = ladder.astype(jnp.bfloat16) * masks_ref[irrep][:cols]
        if (a + 1) % chunk == 0:
            copy(a // chunk).start()

    @pl.loop(0, rows // chunk)
    def _(c):
        copy(c).wait()


def solution(mesh):
    n_row, n_col = mesh.shape["row"], mesh.shape["col"]

    def body(amplitudes, integrals, irrep_sizes, pair_irrep):
        rows, cols, depth = integrals.shape
        n_irrep = irrep_sizes.shape[0]
        n_pairs = pair_irrep.shape[0]
        half = n_pairs // 2
        block = amplitudes.shape[0]
        padded = (cols + 15) // 16 * 16
        vmem, smem = pl.BlockSpec(memory_space=pltpu.VMEM), pl.BlockSpec(memory_space=pltpu.SMEM)
        hbm = pl.BlockSpec(memory_space=pltpu.HBM)
        dma, regular = pltpu.SemaphoreType.DMA, pltpu.SemaphoreType.REGULAR
        inputs = [
            pltpu.with_memory_space_constraint(x, pltpu.HBM)
            for x in (amplitudes, integrals, irrep_sizes, pair_irrep)
        ]
        other, own, weights, masks, ends = pl.pallas_call(
            functools.partial(exchange_kernel, n_row, n_col),
            out_shape=(
                pltpu.VMEM(integrals.shape, jnp.bfloat16),
                pltpu.VMEM(integrals.shape, jnp.bfloat16),
                pltpu.VMEM((2 * depth, half), jnp.bfloat16),
                pltpu.VMEM((n_irrep, padded, half), jnp.bfloat16),
                pltpu.SMEM((n_irrep,), jnp.int32),
            ),
            in_specs=[hbm] * 4,
            out_specs=(vmem,) * 4 + (smem,),
            scratch_shapes=[
                pltpu.VMEM((block, depth), jnp.bfloat16),
                pltpu.SMEM((n_irrep,), jnp.int32),
                pltpu.VMEM((n_pairs,), jnp.int32),
                pltpu.VMEM((2 * block, depth), jnp.float32),
                pltpu.VMEM((2 * block, depth), jnp.bfloat16),
                pltpu.VMEM((n_pairs, depth), jnp.bfloat16),
                regular, regular, dma, dma, dma, dma((3,)),
                dma, dma, dma((n_row * n_col // 2,)), dma((n_row * n_col // 2,)),
            ],
            compiler_params=pltpu.CompilerParams(
                collective_id=0, has_side_effects=True, vmem_limit_bytes=24 << 20
            ),
            name="exchange",
        )(*inputs)
        chunk = 5
        return pl.pallas_call(
            functools.partial(ladder_kernel, chunk),
            out_shape=jax.ShapeDtypeStruct((rows, cols, half), jnp.bfloat16),
            in_specs=[vmem, vmem, vmem, vmem, smem],
            out_specs=hbm,
            scratch_shapes=[pltpu.VMEM((rows, cols, half), jnp.bfloat16), dma((rows // chunk,))],
            compiler_params=pltpu.CompilerParams(vmem_limit_bytes=24 << 20),
            name="ladder",
        )(own, other, weights, masks, ends)

    return jax.shard_map(
        body,
        mesh=mesh,
        in_specs=(P(("row", "col"), "pair"), P("row", "col", "pair"), P(), P()),
        out_specs=P("row", "col", "pair"),
        check_vma=False,
    )
```

```python
import functools

import jax
import jax.numpy as jnp
from jax import lax
from jax.experimental import pallas as pl
from jax.experimental.pallas import tpu as pltpu
from jax.sharding import PartitionSpec as P

MESH = pl.DeviceIdType.MESH


def exchange_kernel(
    n_row, n_col, amp_hbm, integ_ref, sizes_hbm, pairs_hbm,
    other_ref, own_ref, weights_ref, masks_ref, ends_ref,
    amp_ref, sizes_ref, pairs_ref, chip_block, packed, factors,
    ready, go, slab_send, slab_recv, own_sem, in_sems, swap_send, swap_recv, wide_send, wide_recv,
):
    row, col, pair = lax.axis_index("row"), lax.axis_index("col"), lax.axis_index("pair")
    partner = (row, col, 1 - pair)
    block, depth = amp_ref.shape
    half_rows = n_row // 2
    n_slots = half_rows * n_col
    tall = 2 * block
    target_pair = row // half_rows
    slot = lax.rem(row, half_rows) * n_col + col

    barrier = pltpu.get_barrier_semaphore()

    @pl.when(pair == 0)
    def _():
        pl.semaphore_signal(barrier, inc=1, device_id=partner, device_id_type=MESH)

    fetches = [
        pltpu.make_async_copy(amp_hbm, amp_ref, in_sems.at[0]),
        pltpu.make_async_copy(sizes_hbm, sizes_ref, in_sems.at[1]),
        pltpu.make_async_copy(pairs_hbm, pairs_ref, in_sems.at[2]),
    ]
    for fetch in fetches:
        fetch.start()

    for m in range(half_rows):
        for o in range(n_col):
            source_row = pair * half_rows + lax.rem(row + m, half_rows)
            source = (source_row, lax.rem(col + o, n_col), 0)

            def tell():
                pl.semaphore_signal(barrier, inc=1, device_id=source, device_id_type=MESH)

            if m == 0 and o == 0:
                pl.when(target_pair != pair)(tell)
            else:
                tell()

    @pl.when(pair == 1)
    def _():
        pl.semaphore_wait(barrier, 1)
        pl.semaphore_signal(ready, inc=1, device_id=partner, device_id_type=MESH)

    @pl.when(pair == 0)
    def _():
        pl.semaphore_wait(ready, 1)

    slab = pltpu.make_async_remote_copy(
        integ_ref, other_ref, slab_send, slab_recv, device_id=partner, device_id_type=MESH
    )
    slab.start()

    fetches[0].wait()
    mine = pl.ds(pl.multiple_of(pair * block, block), block)
    chip_block[mine] = amp_ref[...].astype(jnp.float32)
    swap = pltpu.make_async_remote_copy(
        chip_block.at[mine], chip_block.at[mine], swap_send, swap_recv, device_id=partner, device_id_type=MESH
    )
    swap.start()

    own_copy = pltpu.make_async_copy(integ_ref, own_ref, own_sem)
    own_copy.start()

    swap.wait_recv()
    packed[...] = chip_block[...].astype(jnp.bfloat16)

    @pl.when(pair == 0)
    def _():
        pl.semaphore_wait(barrier, n_row * n_col - 1)
        pl.semaphore_signal(go, inc=1, device_id=partner, device_id_type=MESH)

    @pl.when(pair == 1)
    def _():
        pl.semaphore_wait(go, 1)

    def place(s):
        return factors.at[pl.ds(pl.multiple_of(s * tall, tall), tall)]

    def wide(i):
        d_row, d_col = i // (n_col // 2), 2 * (i % (n_col // 2))
        target = (lax.rem(row + d_row, n_row), lax.rem(col + pair + d_col, n_col), target_pair)
        return pltpu.make_async_remote_copy(
            packed, place(slot), wide_send.at[i], wide_recv.at[slot], device_id=target, device_id_type=MESH
        )

    n_targets = n_row * n_col // 2
    for i in range(1, n_targets):
        wide(i).start()

    @pl.when(jnp.logical_or(pair == 1, target_pair == 1))
    def _():
        wide(0).start()

    @pl.when(jnp.logical_and(pair == 0, target_pair == 0))
    def _():
        place(slot)[...] = packed[...]

    for fetch in fetches[1:]:
        fetch.wait()
    half = weights_ref.shape[1]
    rows, cols = masks_ref.shape[1], masks_ref.shape[2]
    orbital = col * integ_ref.shape[1] + lax.broadcasted_iota(jnp.int32, (rows, cols), 0)
    irrep = jnp.zeros((rows, cols), jnp.int32)
    end = jnp.int32(0)
    for j in range(masks_ref.shape[0]):
        end = end + sizes_ref[j]
        ends_ref[j] = end
        irrep = irrep + (orbital >= end).astype(jnp.int32)
    wanted = irrep ^ pairs_ref[pl.ds(pl.multiple_of(pair * half, half), half)][None, :]
    for i in range(masks_ref.shape[0]):
        masks_ref[i] = jnp.where(wanted == i, 0.5, 0.0).astype(jnp.bfloat16)

    for s in range(n_slots):

        def arrive():
            pltpu.make_async_remote_copy(
                packed, place(s), wide_send.at[0], wide_recv.at[s], device_id=partner, device_id_type=MESH
            ).wait_recv()

        here = jnp.logical_and(jnp.logical_and(pair == 0, target_pair == 0), slot == s)
        pl.when(jnp.logical_not(here))(arrive)

    both = factors[...].astype(jnp.float32).reshape(n_slots, 2, block, depth)
    for k in range(2):
        part = both[:, k].reshape(half, depth).T.astype(jnp.bfloat16)
        weights_ref[pl.ds(pl.multiple_of(lax.rem(pair + k, 2) * depth, depth), depth)] = part

    swap.wait_send()
    for i in range(1, n_targets):
        wide(i).wait_send()

    @pl.when(jnp.logical_or(pair == 1, target_pair == 1))
    def _():
        wide(0).wait_send()

    own_copy.wait()
    slab.wait()


def ladder_kernel(chunk, own_ref, other_ref, weights_ref, masks_ref, ends_ref, out_ref, staged, sems):
    rows, cols = own_ref.shape[0], own_ref.shape[1]
    first = lax.axis_index("row") * rows
    ends = [ends_ref[j] for j in range(masks_ref.shape[0])]

    def copy(c):
        span = pl.ds(c * chunk, chunk)
        return pltpu.make_async_copy(staged.at[span], out_ref.at[span], sems.at[c])

    for a in range(rows):
        irrep = jnp.int32(0)
        for e in ends:
            irrep = irrep + (first + a >= e).astype(jnp.int32)
        slab = jnp.concatenate([own_ref[a], other_ref[a]], axis=1)
        ladder = jnp.dot(slab, weights_ref[...], preferred_element_type=jnp.float32)
        staged[a] = ladder.astype(jnp.bfloat16) * masks_ref[irrep][:cols]
        if (a + 1) % chunk == 0:
            copy(a // chunk).start()

    @pl.loop(0, rows // chunk)
    def _(c):
        copy(c).wait()


def solution(mesh):
    n_row, n_col = mesh.shape["row"], mesh.shape["col"]

    def body(amplitudes, integrals, irrep_sizes, pair_irrep):
        rows, cols, depth = integrals.shape
        n_irrep = irrep_sizes.shape[0]
        n_pairs = pair_irrep.shape[0]
        half = n_pairs // 2
        block = amplitudes.shape[0]
        padded = (cols + 15) // 16 * 16
        vmem, smem = pl.BlockSpec(memory_space=pltpu.VMEM), pl.BlockSpec(memory_space=pltpu.SMEM)
        hbm = pl.BlockSpec(memory_space=pltpu.HBM)
        dma, regular = pltpu.SemaphoreType.DMA, pltpu.SemaphoreType.REGULAR
        inputs = [
            pltpu.with_memory_space_constraint(x, pltpu.HBM)
            for x in (amplitudes, integrals, irrep_sizes, pair_irrep)
        ]
        other, own, weights, masks, ends = pl.pallas_call(
            functools.partial(exchange_kernel, n_row, n_col),
            out_shape=(
                pltpu.VMEM(integrals.shape, jnp.bfloat16),
                pltpu.VMEM(integrals.shape, jnp.bfloat16),
                pltpu.VMEM((2 * depth, half), jnp.bfloat16),
                pltpu.VMEM((n_irrep, padded, half), jnp.bfloat16),
                pltpu.SMEM((n_irrep,), jnp.int32),
            ),
            in_specs=[hbm] * 4,
            out_specs=(vmem,) * 4 + (smem,),
            scratch_shapes=[
                pltpu.VMEM((block, depth), jnp.bfloat16),
                pltpu.SMEM((n_irrep,), jnp.int32),
                pltpu.VMEM((n_pairs,), jnp.int32),
                pltpu.VMEM((2 * block, depth), jnp.float32),
                pltpu.VMEM((2 * block, depth), jnp.bfloat16),
                pltpu.VMEM((n_pairs, depth), jnp.bfloat16),
                regular, regular, dma, dma, dma, dma((3,)),
                dma, dma, dma((n_row * n_col // 2,)), dma((n_row * n_col // 2,)),
            ],
            compiler_params=pltpu.CompilerParams(
                collective_id=0, has_side_effects=True, vmem_limit_bytes=24 << 20
            ),
            name="exchange",
        )(*inputs)
        chunk = 5
        return pl.pallas_call(
            functools.partial(ladder_kernel, chunk),
            out_shape=jax.ShapeDtypeStruct((rows, cols, half), jnp.bfloat16),
            in_specs=[vmem, vmem, vmem, vmem, smem],
            out_specs=hbm,
            scratch_shapes=[pltpu.VMEM((rows, cols, half), jnp.bfloat16), dma((rows // chunk,))],
            compiler_params=pltpu.CompilerParams(vmem_limit_bytes=24 << 20),
            name="ladder",
        )(own, other, weights, masks, ends)

    return jax.shard_map(
        body,
        mesh=mesh,
        in_specs=(P(("row", "col"), "pair"), P("row", "col", "pair"), P(), P()),
        out_specs=P("row", "col", "pair"),
        check_vma=False,
    )
```

```python
import functools

import jax
import jax.numpy as jnp
from jax import lax
from jax.experimental import pallas as pl
from jax.experimental.pallas import tpu as pltpu
from jax.sharding import PartitionSpec as P

MESH = pl.DeviceIdType.MESH


def exchange_kernel(
    n_row, n_col, amp_hbm, integ_ref, sizes_hbm, pairs_hbm,
    other_ref, own_ref, weights_ref, masks_ref, ends_ref,
    amp_ref, sizes_ref, pairs_ref, chip_block, packed, factors,
    ready, go, slab_send, slab_recv, own_sem, in_sems, swap_send, swap_recv, wide_send, wide_recv,
):
    row, col, pair = lax.axis_index("row"), lax.axis_index("col"), lax.axis_index("pair")
    partner = (row, col, 1 - pair)
    block, depth = amp_ref.shape
    half_rows = n_row // 2
    n_slots = half_rows * n_col
    tall = 2 * block
    target_pair = row // half_rows
    slot = lax.rem(row, half_rows) * n_col + col

    barrier = pltpu.get_barrier_semaphore()

    fetches = [
        pltpu.make_async_copy(amp_hbm, amp_ref, in_sems.at[0]),
        pltpu.make_async_copy(sizes_hbm, sizes_ref, in_sems.at[1]),
        pltpu.make_async_copy(pairs_hbm, pairs_ref, in_sems.at[2]),
    ]
    fetches[0].start()

    @pl.when(pair == 0)
    def _():
        pl.semaphore_signal(barrier, inc=1, device_id=partner, device_id_type=MESH)

    for fetch in fetches[1:]:
        fetch.start()

    for m in range(half_rows):
        for o in range(n_col):
            source_row = pair * half_rows + lax.rem(row + m, half_rows)
            source = (source_row, lax.rem(col + o, n_col), 0)

            def tell():
                pl.semaphore_signal(barrier, inc=1, device_id=source, device_id_type=MESH)

            if m == 0 and o == 0:
                pl.when(target_pair != pair)(tell)
            else:
                tell()

    @pl.when(pair == 1)
    def _():
        pl.semaphore_wait(barrier, 1)
        pl.semaphore_signal(ready, inc=1, device_id=partner, device_id_type=MESH)

    @pl.when(pair == 0)
    def _():
        pl.semaphore_wait(ready, 1)

    slab = pltpu.make_async_remote_copy(
        integ_ref, other_ref, slab_send, slab_recv, device_id=partner, device_id_type=MESH
    )

    fetches[0].wait()
    mine = pl.ds(pl.multiple_of(pair * block, block), block)
    chip_block[mine] = amp_ref[...].astype(jnp.float32)
    swap = pltpu.make_async_remote_copy(
        chip_block.at[mine], chip_block.at[mine], swap_send, swap_recv, device_id=partner, device_id_type=MESH
    )
    swap.start()
    slab.start()


    swap.wait_recv()
    packed[...] = chip_block[...].astype(jnp.bfloat16)

    @pl.when(pair == 0)
    def _():
        pl.semaphore_wait(barrier, n_row * n_col - 1)
        pl.semaphore_signal(go, inc=1, device_id=partner, device_id_type=MESH)

    @pl.when(pair == 1)
    def _():
        pl.semaphore_wait(go, 1)

    def place(s):
        return factors.at[pl.ds(pl.multiple_of(s * tall, tall), tall)]

    def wide(i):
        d_row, d_col = i // (n_col // 2), 2 * (i % (n_col // 2))
        target_row = d_row // half_rows * half_rows + lax.rem(row + d_row, half_rows)
        target = (target_row, lax.rem(col + pair + d_col, n_col), target_pair)
        return pltpu.make_async_remote_copy(
            packed, place(slot), wide_send.at[i], wide_recv.at[slot], device_id=target, device_id_type=MESH
        )

    n_targets = n_row * n_col // 2
    def each_target(act):
        for i in range(n_targets):
            if i == 0:
                pl.when(jnp.logical_or(pair == 1, target_pair == 1))(functools.partial(act, wide(i)))
            else:
                act(wide(i))

    each_target(lambda copy: copy.start())

    @pl.when(jnp.logical_and(pair == 0, target_pair == 0))
    def _():
        place(slot)[...] = packed[...]

    own_copy = pltpu.make_async_copy(integ_ref, own_ref, own_sem)
    own_copy.start()

    for fetch in fetches[1:]:
        fetch.wait()
    half = weights_ref.shape[1]
    rows, cols = masks_ref.shape[1], masks_ref.shape[2]
    orbital = col * integ_ref.shape[1] + lax.broadcasted_iota(jnp.int32, (rows, cols), 0)
    irrep = jnp.zeros((rows, cols), jnp.int32)
    end = jnp.int32(0)
    for j in range(masks_ref.shape[0]):
        end = end + sizes_ref[j]
        ends_ref[j] = end
        irrep = irrep + (orbital >= end).astype(jnp.int32)
    wanted = irrep ^ pairs_ref[pl.ds(pl.multiple_of(pair * half, half), half)][None, :]
    for i in range(masks_ref.shape[0]):
        masks_ref[i] = jnp.where(wanted == i, 0.5, 0.0).astype(jnp.bfloat16)

    parts = 2
    for h in range(parts):
        for s in range(h * n_slots // parts, (h + 1) * n_slots // parts):

            def arrive():
                pltpu.make_async_remote_copy(
                    packed, place(s), wide_send.at[0], wide_recv.at[s], device_id=partner, device_id_type=MESH
                ).wait_recv()

            here = jnp.logical_and(jnp.logical_and(pair == 0, target_pair == 0), slot == s)
            pl.when(jnp.logical_not(here))(arrive)
        span = n_slots // parts * tall
        both = factors[h * span : (h + 1) * span].astype(jnp.float32).reshape(n_slots // parts, 2, block, depth)
        width = half // parts
        for k in range(2):
            part = both[:, k].reshape(width, depth).T.astype(jnp.bfloat16)
            below = pl.ds(pl.multiple_of(lax.rem(pair + k, 2) * depth, depth), depth)
            weights_ref[below, h * width : (h + 1) * width] = part

    swap.wait_send()
    each_target(lambda copy: copy.wait_send())
    own_copy.wait()
    slab.wait()


def ladder_kernel(chunk, own_ref, other_ref, weights_ref, masks_ref, ends_ref, out_ref, staged, sems):
    rows, cols = own_ref.shape[0], own_ref.shape[1]
    first = lax.axis_index("row") * rows
    ends = [ends_ref[j] for j in range(masks_ref.shape[0])]

    def copy(c):
        span = pl.ds(c * chunk, chunk)
        return pltpu.make_async_copy(staged.at[span], out_ref.at[span], sems.at[c])

    for a in range(rows):
        irrep = jnp.int32(0)
        for e in ends:
            irrep = irrep + (first + a >= e).astype(jnp.int32)
        slab = jnp.concatenate([own_ref[a], other_ref[a]], axis=1)
        ladder = jnp.dot(slab, weights_ref[...], preferred_element_type=jnp.float32)
        staged[a] = ladder.astype(jnp.bfloat16) * masks_ref[irrep][:cols]
        if (a + 1) % chunk == 0:
            copy(a // chunk).start()

    @pl.loop(0, rows // chunk)
    def _(c):
        copy(c).wait()


def solution(mesh):
    n_row, n_col = mesh.shape["row"], mesh.shape["col"]

    def body(amplitudes, integrals, irrep_sizes, pair_irrep):
        rows, cols, depth = integrals.shape
        n_irrep = irrep_sizes.shape[0]
        n_pairs = pair_irrep.shape[0]
        half = n_pairs // 2
        block = amplitudes.shape[0]
        padded = (cols + 15) // 16 * 16
        vmem, smem = pl.BlockSpec(memory_space=pltpu.VMEM), pl.BlockSpec(memory_space=pltpu.SMEM)
        hbm = pl.BlockSpec(memory_space=pltpu.HBM)
        dma, regular = pltpu.SemaphoreType.DMA, pltpu.SemaphoreType.REGULAR
        inputs = [
            pltpu.with_memory_space_constraint(x, pltpu.HBM)
            for x in (amplitudes, integrals, irrep_sizes, pair_irrep)
        ]
        other, own, weights, masks, ends = pl.pallas_call(
            functools.partial(exchange_kernel, n_row, n_col),
            out_shape=(
                pltpu.VMEM(integrals.shape, jnp.bfloat16),
                pltpu.VMEM(integrals.shape, jnp.bfloat16),
                pltpu.VMEM((2 * depth, half), jnp.bfloat16),
                pltpu.VMEM((n_irrep, padded, half), jnp.bfloat16),
                pltpu.SMEM((n_irrep,), jnp.int32),
            ),
            in_specs=[hbm] * 4,
            out_specs=(vmem,) * 4 + (smem,),
            scratch_shapes=[
                pltpu.VMEM((block, depth), jnp.bfloat16),
                pltpu.SMEM((n_irrep,), jnp.int32),
                pltpu.VMEM((n_pairs,), jnp.int32),
                pltpu.VMEM((2 * block, depth), jnp.float32),
                pltpu.VMEM((2 * block, depth), jnp.bfloat16),
                pltpu.VMEM((n_pairs, depth), jnp.bfloat16),
                regular, regular, dma, dma, dma, dma((3,)),
                dma, dma, dma((n_row * n_col // 2,)), dma((n_row * n_col // 2,)),
            ],
            compiler_params=pltpu.CompilerParams(
                collective_id=0, has_side_effects=True, vmem_limit_bytes=24 << 20
            ),
            name="exchange",
        )(*inputs)
        chunk = 5
        return pl.pallas_call(
            functools.partial(ladder_kernel, chunk),
            out_shape=jax.ShapeDtypeStruct((rows, cols, half), jnp.bfloat16),
            in_specs=[vmem, vmem, vmem, vmem, smem],
            out_specs=hbm,
            scratch_shapes=[pltpu.VMEM((rows, cols, half), jnp.bfloat16), dma((rows // chunk,))],
            compiler_params=pltpu.CompilerParams(vmem_limit_bytes=24 << 20),
            name="ladder",
        )(own, other, weights, masks, ends)

    return jax.shard_map(
        body,
        mesh=mesh,
        in_specs=(P(("row", "col"), "pair"), P("row", "col", "pair"), P(), P()),
        out_specs=P("row", "col", "pair"),
        check_vma=False,
    )
```
